128 devices in a mesh: replica: 8 (over x, z_lo), section: 8 (over y, z_hi), tensor: 2 (over core).
Axes of the slice: x: 4, y: 4, z: 4 (z_hi: 2, z_lo: 2; z = z_hi * 2 + z_lo), core: 2. Of those that a mesh axis runs over, the one named last changes fastest.
Arguments:
- base_weights: bfloat16 [8, 8192, 512], P('section', None, 'tensor'), may hold values from -6 to 6
- local_weights: bfloat16 [8, 8, 8192, 512], P('replica', 'section', None, 'tensor'), may hold values from -6 to 6
- outer_momentum: float32 [8, 8192, 512], P('section', 'replica', 'tensor'), may hold values from -6 to 6
- scale_exponents: int32 [8, 256, 512], P('section', None, 'tensor'), may hold values from -1 to 1
- section_inputs: bfloat16 [8, 8, 1280, 8192], P('replica', 'section', 'tensor'), may hold values from -6 to 6
- norm_gain: float32 [8, 8192], P('section'), may hold values from 0.1 to 1.9
Outputs:
- new_base: bfloat16 [8, 8192, 512], P('section', None, 'tensor')
- new_momentum: float32 [8, 8192, 512], P('section', 'replica', 'tensor')
- key_out: bfloat16 [8, 8, 1280, 512], P('replica', 'section', 'tensor')
The draws below stay inside these ranges and needn't reach their ends.
All inputs are finite; a program needn't handle non-finite values.
Results may differ from the reference program's by a relative error of at most 0.0049.
Values may be sent and summed in bfloat16 or wider, within the bound.
A program may use at most 192 MiB of HBM per device.

```python
import jax
import jax.numpy as jnp
from jax import lax

D = 8192
TOK = 1280
REPLICAS = 8
SECTIONS = 8
KV = 512
BLOCKS = 256


def with_ends(values, rng, low, high):
    dims = values.shape
    index_at = [jax.random.randint(jax.random.fold_in(rng, axis), (), 0, dims[axis]) for axis in range(len(dims))]
    values = values.at[tuple(index_at)].set(low)
    longest = dims.index(max(dims))
    index_at[longest] = (index_at[longest] + 1) % dims[longest]
    return values.at[tuple(index_at)].set(high)


def steps_of(stream_key, shape, cuts, least, top_value):
    level = 1.0
    for position, parts in cuts:
        steps = jax.random.uniform(jax.random.fold_in(jax.random.fold_in(stream_key, 6), position), (parts,), jnp.float32, least / len(cuts), top_value / len(cuts))
        level = level * jnp.repeat(jnp.exp(steps), shape[position] // parts).reshape((-1,) + (1,) * (len(shape) - 1 - position))
    return level


def noise(key, extent, deviation, reach, pieces=(), kind=jnp.bfloat16):
    entries = deviation * jax.random.normal(key, extent, jnp.float32)
    if pieces:
        entries = entries * steps_of(key, extent, pieces, -0.22, 0.18)
    return jnp.clip(entries, -reach, reach).astype(kind)


def setup_inputs(seed: int = 0) -> dict:
    seeds = jax.random.split(jax.random.key(seed), 7)
    base_weights = noise(seeds[0], (SECTIONS, D, KV), 1.0, 6.0, ((0, 8), (2, 2)))
    local_weights = noise(seeds[1], (REPLICAS, SECTIONS, D, KV), 1.0, 6.0, ((0, 8), (1, 8), (3, 2)))
    outer_momentum = noise(seeds[2], (SECTIONS, D, KV), 1.0, 6.0, ((0, 8), (1, 8), (2, 2)), jnp.float32)
    scale_exponents = with_ends(jax.random.randint(seeds[3], (SECTIONS, BLOCKS, KV), -1, 2), jax.random.fold_in(seeds[3], 1), -1, 1).astype(jnp.int32)
    section_inputs = noise(seeds[4], (REPLICAS, SECTIONS, TOK, D), 1.0, 6.0, ((0, 8), (1, 8), (2, 2)))
    norm_gain = jnp.clip(1.0 + 0.18 * jax.random.normal(seeds[5], (SECTIONS, D), jnp.float32), 0.1, 1.9)
    return dict(base_weights=base_weights, local_weights=local_weights, outer_momentum=outer_momentum, scale_exponents=scale_exponents, section_inputs=section_inputs, norm_gain=norm_gain)


OUTER_RATE = 0.7
MOMENTUM_DECAY = 0.9
NORM_EPSILON = 1e-05

def quantize(deltas, exponents):
    scales = jnp.where(exponents < 0, 0.5, jnp.where(exponents > 0, 2.0, 1.0)).astype(jnp.float32)
    blocked = deltas.reshape(exponents.shape[0], 32, exponents.shape[1])
    scaled = blocked / scales[:, None, :]
    magnitude = jnp.minimum(jnp.abs(scaled), 6.0)
    spacing = jnp.where(magnitude < 2.0, 0.5, jnp.where(magnitude < 4.0, 1.0, 2.0))
    levels = jnp.floor(magnitude / spacing + 0.5) * spacing
    signed = jnp.sign(scaled) * levels * scales[:, None, :]
    return signed.reshape(deltas.shape)

def outer_section(inputs):
    base_layer, local_layer, moment, exponents = inputs
    base_f = base_layer.astype(jnp.float32)

    def one_replica(weights):
        return quantize(base_f - weights.astype(jnp.float32), exponents)
    summed = lax.optimization_barrier(jnp.sum(lax.map(one_replica, local_layer), axis=0))
    pseudo = summed / REPLICAS
    moment_new = MOMENTUM_DECAY * moment + pseudo
    updated = (base_f - OUTER_RATE * (pseudo + MOMENTUM_DECAY * moment_new)).astype(jnp.bfloat16)
    return (updated, moment_new)

def replica_keys(inputs):
    activations, weights, norm_gain = inputs
    passed = jnp.roll(activations, 1, axis=0).astype(jnp.float32)
    meansq = lax.optimization_barrier(jnp.mean(passed * passed, axis=-1, keepdims=True))
    normed = (passed * lax.rsqrt(meansq + NORM_EPSILON) * norm_gain[:, None, :]).astype(jnp.bfloat16)
    product = jnp.einsum('std,sdk->stk', normed.astype(jnp.float32), weights.astype(jnp.float32))
    return (product * D ** (-0.5)).astype(jnp.bfloat16)

def reference(base_weights, local_weights, outer_momentum, scale_exponents, section_inputs, norm_gain):
    local_by_section = jnp.swapaxes(local_weights, 0, 1)
    new_base, new_momentum = lax.map(outer_section, (base_weights, local_by_section, outer_momentum, scale_exponents))
    key_out = lax.map(lambda pair: replica_keys((pair[0], pair[1], norm_gain)), (section_inputs, local_weights))
    return (new_base, new_momentum, key_out)
```

```python
import jax
import jax.numpy as jnp
from jax import lax
from jax.experimental import pallas as pl
from jax.experimental.pallas import tpu as pltpu
from jax.sharding import PartitionSpec as P

MESH = pl.DeviceIdType.MESH
D = 8192
TOK = 640
KV = 256
LANES = 128
REPLICAS = 8
ROWS = D // REPLICAS
J = 4
JR = ROWS // J
NK = 8
KR = D // NK
NW = 2 * NK
XP = 4
XR = TOK // XP
NR = 32
MR = TOK // 2

OUTER_RATE = 0.7
MOMENTUM_DECAY = 0.9
NORM_EPSILON = 1e-05


def schedule():
    events = []
    for j in range(J):
        summed = 16 + 14 * j
        events += [(summed, "sum", j), (summed + 17, "update", j), (summed + 34, "pass", j)]
    events += [(14 + 7 * i, "weights", i) for i in range(NW)]
    return [(name, i) for _, name, i in sorted(events)]


def kernel(
    base, local, moment, exps, acts, gain,
    base_out, moment_out, keys_out,
    bbuf, qbuf, ebuf, mbuf, xbuf, gbuf, wbuf, rbuf, pbuf, zbuf, nbuf, acc, kbuf,
    load_b, load_q, load_e, load_m, load_x, store_n, store_m,
    g_send, g_recv, w_send, w_recv, f_send, f_recv, r_send, r_recv, z_send, z_recv,
    a_send, a_recv, o_send, o_recv, p_send, p_recv, k_send, k_recv,
):
    r, s, t = lax.axis_index("replica"), lax.axis_index("section"), lax.axis_index("tensor")
    x, zl = r // 2, r % 2
    before, after = (r, (s + 7) % 8, t), (r, (s + 1) % 8, t)
    sibling = (r, s, 1 - t)
    rz = x * 2 + 1 - zl
    pair = (rz, s, t)
    others = [(((x + d) % 4) * 2 + zl, s, t) for d in (1, 2, 3)]

    def rows(j):
        return pl.ds(j * JR, JR)

    def remote(src, dst, send, recv, to):
        return pltpu.make_async_remote_copy(
            src_ref=src, dst_ref=dst, send_sem=send, recv_sem=recv, device_id=to, device_id_type=MESH
        )

    def weights_copy(i):
        b, k = i // NK, i % NK
        cols = pl.ds(pl.multiple_of(b * LANES, LANES), LANES)
        deep = pl.ds(pl.multiple_of(k * KR, KR), KR)
        return remote(local.at[deep, cols], wbuf.at[b, t, deep], w_send.at[i], w_recv.at[i], before)

    def share_copy(i, core):
        b, k = i // NK, i % NK
        deep = pl.ds(pl.multiple_of(k * KR, KR), KR)
        ref = wbuf.at[b, core, deep]
        return remote(ref, ref, f_send.at[i], f_recv.at[i], sibling)

    gain_copy = remote(gain, gbuf, g_send, g_recv, before)

    def term_copy(j, d):
        xd = (x + d + 1) % 4
        return remote(
            qbuf.at[pl.ds(xd * 2, 2), rows(j)], rbuf.at[d, :, rows(j)],
            r_send.at[j, d], r_recv.at[j, d], others[d],
        )

    def half_copy(j):
        return remote(pbuf.at[1 - zl, rows(j)], zbuf.at[rows(j)], z_send.at[j], z_recv.at[j], pair)

    def pair_copy(j):
        return remote(nbuf.at[rows(j)], base_out.at[r, rows(j)], a_send.at[j], a_recv.at[j], pair)

    def own_copy(j, d):
        return remote(
            nbuf.at[rows(j)], base_out.at[r, rows(j)], o_send.at[j, d], o_recv.at[j, d], others[d]
        )

    def pass_copy(j, d):
        ref = base_out.at[rz, rows(j)]
        return remote(ref, ref, p_send.at[j, d], p_recv.at[j, d], others[d])

    def key_copy(b, c):
        return remote(
            kbuf.at[b, c], keys_out.at[:, pl.ds(c * KV + b * LANES, LANES)],
            k_send.at[b, c], k_recv.at[b, c], after,
        )

    def store_copy(j):
        return pltpu.make_async_copy(nbuf.at[rows(j)], base_out.at[r, rows(j)], store_n.at[j])

    store_moment = pltpu.make_async_copy(mbuf, moment_out, store_m)

    def load_base(j):
        return pltpu.make_async_copy(base.at[:, rows(j)], bbuf.at[:, rows(j)], load_b.at[j])

    local3 = local.reshape(REPLICAS, ROWS, KV)

    def load_local(j):
        return pltpu.make_async_copy(local3.at[:, rows(j)], qbuf.at[:, rows(j)], load_q.at[j])

    load_exps = pltpu.make_async_copy(exps, ebuf, load_e)
    load_moment = pltpu.make_async_copy(moment, mbuf, load_m)

    def load_acts(i):
        part = pl.ds(i * XR, XR)
        return pltpu.make_async_copy(acts.at[part], xbuf.at[part], load_x.at[i])

    load_exps.start()
    for j in range(J):
        load_base(j).start()
        load_local(j).start()
    for i in range(XP):
        load_acts(i).start()
    load_moment.start()

    barrier = pltpu.get_barrier_semaphore()
    for peer in (before, after, sibling, pair, *others):
        pl.semaphore_signal(barrier, inc=1, device_id=peer, device_id_type=MESH)
    pl.semaphore_wait(barrier, 7)

    gain_copy.start()

    @pl.loop(0, NW)
    def _(i):
        weights_copy(i).start()

    load_exps.wait()
    for j in range(J):
        load_base(j).wait()
        load_local(j).wait()

        @pl.loop(0, REPLICAS)
        def _(q):
            e = ebuf[q, pl.ds(j * (JR // 32), JR // 32), :]
            scale = jnp.where(e < 0, 0.5, jnp.where(e > 0, 2.0, 1.0)).astype(jnp.float32)
            inverse = jnp.where(e < 0, 2.0, jnp.where(e > 0, 0.5, 1.0)).astype(jnp.float32)
            delta = bbuf[q, rows(j), :].astype(jnp.float32) - qbuf[q, rows(j), :].astype(jnp.float32)
            y = delta.reshape(JR // 32, 32, KV) * inverse[:, None, :]
            a = jnp.minimum(jnp.abs(y), 6.0)
            spacing = jnp.where(a < 2.0, 0.5, jnp.where(a < 4.0, 1.0, 2.0))
            per = jnp.where(a < 2.0, 2.0, jnp.where(a < 4.0, 1.0, 0.5))
            level = jnp.floor(a * per + 0.5) * spacing * scale[:, None, :]
            level = jnp.where(y < 0.0, -level, level)
            qbuf[q, rows(j), :] = level.reshape(JR, KV).astype(jnp.bfloat16)

        for d in range(3):
            term_copy(j, d).start()

    for i in range(XP):
        load_acts(i).wait()
    gain_copy.wait_recv()

    @pl.loop(0, TOK // NR)
    def _(i):
        part = pl.ds(pl.multiple_of(i * NR, NR), NR)
        total = jnp.zeros((NR, LANES), jnp.float32)
        for k in range(NK):
            v = xbuf[part, k * KR : (k + 1) * KR].astype(jnp.float32)
            v = v * v
            for lane in range(0, KR, LANES):
                total = total + v[:, lane : lane + LANES]
        meansq = jnp.sum(total, axis=-1, keepdims=True) * (1.0 / D)
        factor = lax.rsqrt(meansq + NORM_EPSILON)
        for k in range(NK):
            cols = slice(k * KR, (k + 1) * KR)
            v = xbuf[part, cols].astype(jnp.float32)
            xbuf[part, cols] = (v * factor * gbuf[:, cols]).astype(jnp.bfloat16)

    load_moment.wait()

    def sum_terms(j):
        for d in range(3):
            term_copy(j, d).wait_recv()
        for h in range(2):
            total = qbuf[x * 2 + h, rows(j), :].astype(jnp.float32)
            for d in range(3):
                total = total + rbuf[d, h, rows(j), :].astype(jnp.float32)
            pbuf[h, rows(j), :] = total.astype(jnp.bfloat16)
        half_copy(j).start()

    def update(j):
        half_copy(j).wait_recv()
        total = pbuf[zl, rows(j), :].astype(jnp.float32) + zbuf[rows(j), :].astype(jnp.float32)
        pseudo = total * (1.0 / REPLICAS)
        new = MOMENTUM_DECAY * mbuf[rows(j), :] + pseudo
        mbuf[rows(j), :] = new
        old = bbuf[r, rows(j), :].astype(jnp.float32)
        nbuf[rows(j), :] = (old - OUTER_RATE * (pseudo + MOMENTUM_DECAY * new)).astype(jnp.bfloat16)
        pair_copy(j).start()
        for d in range(3):
            own_copy(j, d).start()
        store_copy(j).start()
        if j == J - 1:
            store_moment.start()

    def pass_on(j):
        pair_copy(j).wait_recv()
        for d in range(3):
            pass_copy(j, d).start()

    def weights(i):
        weights_copy(i).wait_recv()
        share_copy(i, t).start()

    def multiply(first, last):
        @pl.loop(first, last)
        def _(i):
            weights(i)
            share_copy(i, 1 - t).wait_recv()
            b, k = i // NK, i % NK
            deep = pl.ds(pl.multiple_of(k * KR, KR), KR)

            @pl.loop(0, TOK // MR)
            def _(m):
                part = pl.ds(pl.multiple_of(m * MR, MR), MR)
                w = jnp.concatenate([wbuf[b, 0, deep, :], wbuf[b, 1, deep, :]], axis=1)
                product = jnp.dot(xbuf[part, deep], w, preferred_element_type=jnp.float32)
                kept = jnp.where(k == 0, 0.0, acc[part, :])
                acc[part, :] = kept + product

    def keys(b):
        for c in range(2):
            kbuf[b, c] = (acc[:, c * LANES : (c + 1) * LANES] * D ** (-0.5)).astype(jnp.bfloat16)
            key_copy(b, c).start()

    run = []

    def flush():
        if run:
            multiply(run[0], run[-1] + 1)
            if run[-1] % NK == NK - 1:
                keys(run[-1] // NK)
            run.clear()

    for name, i in schedule():
        if name == "weights":
            run.append(i)
            if i % NK == NK - 1:
                flush()
            continue
        flush()
        {"sum": sum_terms, "update": update, "pass": pass_on}[name](i)
    flush()

    gain_copy.wait_send()

    @pl.loop(0, NW)
    def _(i):
        weights_copy(i).wait_send()
        share_copy(i, t).wait_send()

    @pl.loop(0, J)
    def _(j):
        half_copy(j).wait_send()
        pair_copy(j).wait_send()
        store_copy(j).wait()
        for d in range(3):
            term_copy(j, d).wait_send()
            own_copy(j, d).wait()
            pass_copy(j, d).wait()

    store_moment.wait()
    for b in range(2):
        for c in range(2):
            key_copy(b, c).wait()


def shards(base_weights, local_weights, outer_momentum, scale_exponents, section_inputs, norm_gain):
    bf16, f32 = jnp.bfloat16, jnp.float32
    hbm = pl.BlockSpec(memory_space=pl.ANY)
    dma = pltpu.SemaphoreType.DMA
    new_base, new_moment, keys = pl.pallas_call(
        kernel,
        out_shape=(
            jax.ShapeDtypeStruct((REPLICAS, ROWS, KV), bf16),
            jax.ShapeDtypeStruct((ROWS, KV), f32),
            jax.ShapeDtypeStruct((TOK, 2 * KV), bf16),
        ),
        in_specs=[hbm] * 6,
        out_specs=(hbm, hbm, hbm),
        scratch_shapes=[
            pltpu.VMEM((REPLICAS, ROWS, KV), bf16),
            pltpu.VMEM((REPLICAS, ROWS, KV), bf16),
            pltpu.VMEM((REPLICAS, ROWS // 32, KV), jnp.int32),
            pltpu.VMEM((ROWS, KV), f32),
            pltpu.VMEM((TOK, D), bf16),
            pltpu.VMEM((1, D), f32),
            pltpu.VMEM((2, 2, D, LANES), bf16),
            pltpu.VMEM((3, 2, ROWS, KV), bf16),
            pltpu.VMEM((2, ROWS, KV), bf16),
            pltpu.VMEM((ROWS, KV), bf16),
            pltpu.VMEM((ROWS, KV), bf16),
            pltpu.VMEM((TOK, KV), f32),
            pltpu.VMEM((2, 2, TOK, LANES), bf16),
            dma((J,)), dma((J,)), dma, dma, dma((XP,)), dma((J,)), dma,
            dma, dma, dma((NW,)), dma((NW,)), dma((NW,)), dma((NW,)),
            dma((J, 3)), dma((J, 3)), dma((J,)), dma((J,)),
            dma((J,)), dma((J,)), dma((J, 3)), dma((J, 3)), dma((J, 3)), dma((J, 3)),
            dma((2, 2)), dma((2, 2)),
        ],
        compiler_params=pltpu.CompilerParams(
            collective_id=0, has_side_effects=True, vmem_limit_bytes=56 << 20
        ),
        cost_estimate=pl.CostEstimate(
            flops=2 * TOK * D * 2 * KV, bytes_accessed=40 << 20, transcendentals=0
        ),
    )(
        base_weights.reshape(REPLICAS, ROWS, KV),
        local_weights.reshape(D, KV),
        outer_momentum.reshape(ROWS, KV),
        scale_exponents.reshape(REPLICAS, ROWS // 32, KV),
        section_inputs.reshape(TOK, D),
        norm_gain,
    )
    return (
        new_base.reshape(1, D, KV),
        new_moment.reshape(1, ROWS, KV),
        keys.reshape(1, 1, TOK, 2 * KV),
    )


def solution(mesh):
    placed = (
        P("section", None, "tensor"),
        P("replica", "section", None, "tensor"),
        P("section", "replica", "tensor"),
        P("section", None, "tensor"),
        P("replica", "section", "tensor", None),
        P("section", None),
    )
    return jax.shard_map(
        shards,
        mesh=mesh,
        in_specs=placed,
        out_specs=(
            P("section", None, "tensor"),
            P("section", "replica", "tensor"),
            P("replica", "section", "tensor", None),
        ),
        check_vma=False,
    )
```

```python
import jax
import jax.numpy as jnp
from jax import lax
from jax.experimental import pallas as pl
from jax.experimental.pallas import tpu as pltpu
from jax.sharding import PartitionSpec as P

MESH = pl.DeviceIdType.MESH
D = 8192
TOK = 640
KV = 256
LANES = 128
REPLICAS = 8
ROWS = D // REPLICAS
J = 4
JR = ROWS // J
NK = 8
KR = D // NK
NW = 2 * NK
XP = 4
XR = TOK // XP
NR = 32
MR = TOK // 2

OUTER_RATE = 0.7
MOMENTUM_DECAY = 0.9
NORM_EPSILON = 1e-05


EARLY = 10
ORDER = (
    [("relay", 0), ("normalize", 0), ("normalize", 1), ("sum", 0), ("normalize", 2), ("normalize", 3)]
    + [("relay", 1), ("sum", 1), ("weights", 0), ("weights", 1)]
    + [("relay", 2), ("sum", 2), ("weights", 2), ("weights", 3), ("relay", 3), ("sum", 3)]
    + [("send", i) for i in range(EARLY, 13)]
    + [("weights", i) for i in range(4, 8)]
    + [("update", j) for j in range(J)]
    + [("send", i) for i in range(13, NW)]
    + [("hop", j) for j in range(J)]
    + [("weights", i) for i in range(8, 11)]
    + [("pass", j) for j in range(J)]
    + [("hop_pair", j) for j in range(J)]
    + [("weights", i) for i in range(11, NW)]
)


def kernel(
    base, local, moment, exps, acts, gain,
    base_out, moment_out, keys_out,
    bbuf, qbuf, ebuf, mbuf, xbuf, gbuf, wbuf, vbuf, sbuf, dbuf, pbuf, zbuf, nbuf, acc, kbuf,
    load_b, load_q, load_e, load_m, load_x, store_n, store_m,
    g_send, g_recv, w_send, w_recv, f_send, f_recv, v_send, v_recv, s_send, s_recv, d_send, d_recv,
    z_send, z_recv, a_send, a_recv, n_send, n_recv, h_send, h_recv, k_send, k_recv,
):
    r, s, t = lax.axis_index("replica"), lax.axis_index("section"), lax.axis_index("tensor")
    x, zl = r // 2, r % 2
    before, after = (r, (s + 7) % 8, t), (r, (s + 1) % 8, t)
    sibling = (r, s, 1 - t)
    rz = x * 2 + 1 - zl
    pair = (rz, s, t)
    up, down = ((x + 1) % 4) * 2 + zl, ((x + 3) % 4) * 2 + zl
    along = [(up, s, t), (down, s, t)]

    def rows(j):
        return pl.ds(j * JR, JR)

    def remote(src, dst, send, recv, to):
        return pltpu.make_async_remote_copy(
            src_ref=src, dst_ref=dst, send_sem=send, recv_sem=recv, device_id=to, device_id_type=MESH
        )

    def weights_copy(i):
        b, k = i // NK, i % NK
        cols = pl.ds(pl.multiple_of(b * LANES, LANES), LANES)
        deep = pl.ds(pl.multiple_of(k * KR, KR), KR)
        return remote(local.at[deep, cols], wbuf.at[b, t, deep], w_send.at[i], w_recv.at[i], before)

    def share_copy(i, core):
        b, k = i // NK, i % NK
        deep = pl.ds(pl.multiple_of(k * KR, KR), KR)
        ref = wbuf.at[b, core, deep]
        return remote(ref, ref, f_send.at[i], f_recv.at[i], sibling)

    gain_copy = remote(gain, gbuf, g_send, g_recv, before)

    def shard(d):
        return (x + d) % 4 * 2

    def via_copy(j, h):
        return remote(
            qbuf.at[shard(2) + h, rows(j)], vbuf.at[h, rows(j)], v_send.at[h, j], v_recv.at[h, j], along[h]
        )

    def sum_copy(j, h):
        return remote(vbuf.at[h, rows(j)], sbuf.at[h, rows(j)], s_send.at[h, j], s_recv.at[h, j], along[h])

    def term_copy(j, h):
        return remote(
            qbuf.at[shard(3 if h == 0 else 1) + h, rows(j)], dbuf.at[h, rows(j)],
            d_send.at[h, j], d_recv.at[h, j], along[1 - h],
        )

    def half_copy(j):
        return remote(pbuf.at[1 - zl, rows(j)], zbuf.at[rows(j)], z_send.at[j], z_recv.at[j], pair)

    def pair_copy(j):
        return remote(nbuf.at[rows(j)], base_out.at[r, rows(j)], a_send.at[j], a_recv.at[j], pair)

    def own_copy(j, w):
        return remote(
            nbuf.at[rows(j)], base_out.at[r, rows(j)], n_send.at[zl, w, j], n_recv.at[zl, w, j], along[w]
        )

    def pass_copy(j, w):
        ref = base_out.at[rz, rows(j)]
        return remote(ref, ref, n_send.at[1 - zl, w, j], n_recv.at[1 - zl, w, j], along[w])

    def came_copy(j, h, w):
        ref = base_out.at[(x + 3 + 2 * w) % 4 * 2 + h, rows(j)]
        return remote(ref, ref, n_send.at[h, w, j], n_recv.at[h, w, j], along[0])

    def hop_copy(j, h):
        ref = base_out.at[(x + 3 + 2 * h) % 4 * 2 + h, rows(j)]
        to = ((x + 1 + 2 * h) % 4 * 2 + zl, s, t)
        return remote(ref, ref, h_send.at[h, j], h_recv.at[h, j], to)

    def key_copy(b, c):
        return remote(
            kbuf.at[b, c], keys_out.at[:, pl.ds(c * KV + b * LANES, LANES)],
            k_send.at[b, c], k_recv.at[b, c], after,
        )

    def store_copy(j):
        return pltpu.make_async_copy(nbuf.at[rows(j)], base_out.at[r, rows(j)], store_n.at[j])

    store_moment = pltpu.make_async_copy(mbuf, moment_out, store_m)

    def load_base(j):
        return pltpu.make_async_copy(base.at[:, rows(j)], bbuf.at[:, rows(j)], load_b.at[j])

    local3 = local.reshape(REPLICAS, ROWS, KV)

    def load_local(j):
        return pltpu.make_async_copy(local3.at[:, rows(j)], qbuf.at[:, rows(j)], load_q.at[j])

    load_exps = pltpu.make_async_copy(exps, ebuf, load_e)
    load_moment = pltpu.make_async_copy(moment, mbuf, load_m)

    def load_acts(i):
        part = pl.ds(i * XR, XR)
        return pltpu.make_async_copy(acts.at[part], xbuf.at[part], load_x.at[i])

    load_exps.start()
    for j in range(J):
        load_base(j).start()
        load_local(j).start()

    barrier = pltpu.get_barrier_semaphore()
    for peer in (before, after, sibling, pair, *along):
        pl.semaphore_signal(barrier, inc=1, device_id=peer, device_id_type=MESH)
    pl.semaphore_wait(barrier, 6)

    gain_copy.start()

    @pl.loop(0, EARLY)
    def _(i):
        weights_copy(i).start()

    load_exps.wait()
    for j in range(J):
        load_base(j).wait()
        load_local(j).wait()

        @pl.loop(0, REPLICAS)
        def _(q):
            e = ebuf[q, pl.ds(j * (JR // 32), JR // 32), :]
            scale = jnp.where(e < 0, 0.5, jnp.where(e > 0, 2.0, 1.0)).astype(jnp.float32)
            inverse = jnp.where(e < 0, 2.0, jnp.where(e > 0, 0.5, 1.0)).astype(jnp.float32)
            delta = bbuf[q, rows(j), :].astype(jnp.float32) - qbuf[q, rows(j), :].astype(jnp.float32)
            y = delta.reshape(JR // 32, 32, KV) * inverse[:, None, :]
            a = jnp.minimum(jnp.abs(y), 6.0)
            spacing = jnp.where(a < 2.0, 0.5, jnp.where(a < 4.0, 1.0, 2.0))
            per = jnp.where(a < 2.0, 2.0, jnp.where(a < 4.0, 1.0, 0.5))
            level = jnp.floor(a * per + 0.5) * spacing * scale[:, None, :]
            level = jnp.where(y < 0.0, -level, level)
            qbuf[q, rows(j), :] = level.reshape(JR, KV).astype(jnp.bfloat16)

        for h in range(2):
            via_copy(j, h).start()
        for h in range(2):
            term_copy(j, h).start()
        if j == 1:
            for i in range(XP):
                load_acts(i).start()
            load_moment.start()

    def normalize(part_at):
        load_acts(part_at).wait()
        if part_at == 0:
            gain_copy.wait_recv()

        @pl.loop(0, XR // NR)
        def _(i):
            part = pl.ds(pl.multiple_of(part_at * XR + i * NR, NR), NR)
            total = jnp.zeros((NR, LANES), jnp.float32)
            for k in range(NK):
                v = xbuf[part, k * KR : (k + 1) * KR].astype(jnp.float32)
                v = v * v
                for lane in range(0, KR, LANES):
                    total = total + v[:, lane : lane + LANES]
            meansq = jnp.sum(total, axis=-1, keepdims=True) * (1.0 / D)
            factor = lax.rsqrt(meansq + NORM_EPSILON)
            for k in range(NK):
                cols = slice(k * KR, (k + 1) * KR)
                v = xbuf[part, cols].astype(jnp.float32)
                xbuf[part, cols] = (v * factor * gbuf[:, cols]).astype(jnp.bfloat16)

    def relay(j):
        for h in range(2):
            via_copy(j, h).wait_recv()
            mine = qbuf[shard(1 if h == 0 else 3) + h, rows(j), :].astype(jnp.float32)
            vbuf[h, rows(j), :] = (vbuf[h, rows(j), :].astype(jnp.float32) + mine).astype(jnp.bfloat16)
            sum_copy(j, h).start()

    def sum_terms(j):
        for h in range(2):
            term_copy(j, h).wait_recv()
            sum_copy(j, h).wait_recv()
            total = qbuf[x * 2 + h, rows(j), :].astype(jnp.float32)
            total = total + sbuf[h, rows(j), :].astype(jnp.float32) + dbuf[h, rows(j), :].astype(jnp.float32)
            pbuf[h, rows(j), :] = total.astype(jnp.bfloat16)
        half_copy(j).start()

    def update(j):
        if j == 0:
            load_moment.wait()
        half_copy(j).wait_recv()
        total = pbuf[zl, rows(j), :].astype(jnp.float32) + zbuf[rows(j), :].astype(jnp.float32)
        pseudo = total * (1.0 / REPLICAS)
        new = MOMENTUM_DECAY * mbuf[rows(j), :] + pseudo
        mbuf[rows(j), :] = new
        old = bbuf[r, rows(j), :].astype(jnp.float32)
        nbuf[rows(j), :] = (old - OUTER_RATE * (pseudo + MOMENTUM_DECAY * new)).astype(jnp.bfloat16)
        pair_copy(j).start()
        for w in range(2):
            own_copy(j, w).start()
        store_copy(j).start()
        if j == J - 1:
            store_moment.start()

    def pass_on(j):
        pair_copy(j).wait_recv()
        for w in range(2):
            pass_copy(j, w).start()

    def hop(j, h):
        came_copy(j, h, h).wait_recv()
        hop_copy(j, h).start()

    def weights(i):
        weights_copy(i).wait_recv()
        share_copy(i, t).start()

    def multiply(i):
        share_copy(i, 1 - t).wait_recv()
        b, k = i // NK, i % NK
        deep = pl.ds(pl.multiple_of(k * KR, KR), KR)

        @pl.loop(0, TOK // MR)
        def _(m):
            part = pl.ds(pl.multiple_of(m * MR, MR), MR)
            w = jnp.concatenate([wbuf[b, 0, deep, :], wbuf[b, 1, deep, :]], axis=1)
            product = jnp.dot(xbuf[part, deep], w, preferred_element_type=jnp.float32)
            kept = jnp.where(k == 0, 0.0, acc[part, :])
            acc[part, :] = kept + product

    def arrive(first, last):
        if first == 0:
            weights(0)
            first = 1

        @pl.loop(first, last)
        def _(i):
            weights(i)
            multiply(i - 1)

    def keys(b):
        for c in range(2):
            kbuf[b, c] = (acc[:, c * LANES : (c + 1) * LANES] * D ** (-0.5)).astype(jnp.bfloat16)
            key_copy(b, c).start()

    run = []

    def flush():
        if run:
            arrive(run[0], run[-1] + 1)
            if run[-1] == NK:
                keys(0)
            run.clear()

    for name, i in ORDER:
        if name == "weights":
            run.append(i)
            if i == NK:
                flush()
            continue
        flush()
        if name == "send":
            weights_copy(i).start()
        elif name == "hop":
            hop(i, zl)
        elif name == "hop_pair":
            hop(i, 1 - zl)
        else:
            {"normalize": normalize, "relay": relay, "sum": sum_terms, "update": update, "pass": pass_on}[name](i)
    flush()
    multiply(NW - 1)
    keys(1)

    gain_copy.wait_send()

    @pl.loop(0, NW)
    def _(i):
        weights_copy(i).wait_send()
        share_copy(i, t).wait_send()

    @pl.loop(0, J)
    def _(j):
        half_copy(j).wait_send()
        pair_copy(j).wait_send()
        store_copy(j).wait()
        for h in range(2):
            via_copy(j, h).wait_send()
            sum_copy(j, h).wait_send()
            term_copy(j, h).wait_send()
            own_copy(j, h).wait_send()
            pass_copy(j, h).wait_send()
            came_copy(j, h, 1 - h).wait_recv()
            hop_copy(j, h).wait()

    store_moment.wait()
    for b in range(2):
        for c in range(2):
            key_copy(b, c).wait()


def shards(base_weights, local_weights, outer_momentum, scale_exponents, section_inputs, norm_gain):
    bf16, f32 = jnp.bfloat16, jnp.float32
    hbm = pl.BlockSpec(memory_space=pl.ANY)
    dma = pltpu.SemaphoreType.DMA
    new_base, new_moment, keys = pl.pallas_call(
        kernel,
        out_shape=(
            jax.ShapeDtypeStruct((REPLICAS, ROWS, KV), bf16),
            jax.ShapeDtypeStruct((ROWS, KV), f32),
            jax.ShapeDtypeStruct((TOK, 2 * KV), bf16),
        ),
        in_specs=[hbm] * 6,
        out_specs=(hbm, hbm, hbm),
        scratch_shapes=[
            pltpu.VMEM((REPLICAS, ROWS, KV), bf16),
            pltpu.VMEM((REPLICAS, ROWS, KV), bf16),
            pltpu.VMEM((REPLICAS, ROWS // 32, KV), jnp.int32),
            pltpu.VMEM((ROWS, KV), f32),
            pltpu.VMEM((TOK, D), bf16),
            pltpu.VMEM((1, D), f32),
            pltpu.VMEM((2, 2, D, LANES), bf16),
            pltpu.VMEM((2, ROWS, KV), bf16),
            pltpu.VMEM((2, ROWS, KV), bf16),
            pltpu.VMEM((2, ROWS, KV), bf16),
            pltpu.VMEM((2, ROWS, KV), bf16),
            pltpu.VMEM((ROWS, KV), bf16),
            pltpu.VMEM((ROWS, KV), bf16),
            pltpu.VMEM((TOK, KV), f32),
            pltpu.VMEM((2, 2, TOK, LANES), bf16),
            dma((J,)), dma((J,)), dma, dma, dma((XP,)), dma((J,)), dma,
            dma, dma, dma((NW,)), dma((NW,)), dma((NW,)), dma((NW,)),
            dma((2, J)), dma((2, J)), dma((2, J)), dma((2, J)), dma((2, J)), dma((2, J)),
            dma((J,)), dma((J,)), dma((J,)), dma((J,)), dma((2, 2, J)), dma((2, 2, J)), dma((2, J)), dma((2, J)),
            dma((2, 2)), dma((2, 2)),
        ],
        compiler_params=pltpu.CompilerParams(
            collective_id=0, has_side_effects=True, vmem_limit_bytes=56 << 20
        ),
        cost_estimate=pl.CostEstimate(
            flops=2 * TOK * D * 2 * KV, bytes_accessed=40 << 20, transcendentals=0
        ),
    )(
        base_weights.reshape(REPLICAS, ROWS, KV),
        local_weights.reshape(D, KV),
        outer_momentum.reshape(ROWS, KV),
        scale_exponents.reshape(REPLICAS, ROWS // 32, KV),
        section_inputs.reshape(TOK, D),
        norm_gain,
    )
    return (
        new_base.reshape(1, D, KV),
        new_moment.reshape(1, ROWS, KV),
        keys.reshape(1, 1, TOK, 2 * KV),
    )


def solution(mesh):
    placed = (
        P("section", None, "tensor"),
        P("replica", "section", None, "tensor"),
        P("section", "replica", "tensor"),
        P("section", None, "tensor"),
        P("replica", "section", "tensor", None),
        P("section", None),
    )
    return jax.shard_map(
        shards,
        mesh=mesh,
        in_specs=placed,
        out_specs=(
            P("section", None, "tensor"),
            P("section", "replica", "tensor"),
            P("replica", "section", "tensor", None),
        ),
        check_vma=False,
    )
```

```python
import jax
import jax.numpy as jnp
from jax import lax
from jax.experimental import pallas as pl
from jax.experimental.pallas import tpu as pltpu
from jax.sharding import PartitionSpec as P

MESH = pl.DeviceIdType.MESH
D = 8192
TOK = 640
KV = 256
LANES = 128
REPLICAS = 8
ROWS = D // REPLICAS
J = 4
JR = ROWS // J
NK = 8
KR = D // NK
NW = 2 * NK
XP = 4
XR = TOK // XP
NR = 32
MR = TOK // 2

OUTER_RATE = 0.7
MOMENTUM_DECAY = 0.9
NORM_EPSILON = 1e-05


EARLY = 8
ORDER = (
    [("relay", 0), ("normalize", 0), ("normalize", 1), ("sum", 0), ("normalize", 2), ("normalize", 3)]
    + [("relay", 1), ("sum", 1), ("weights", 0), ("weights", 1)]
    + [("relay", 2), ("sum", 2), ("weights", 2), ("weights", 3), ("relay", 3), ("sum", 3)]
    + [("weights", i) for i in range(4, NK)]
    + [("update", j) for j in range(J)]
    + [("odd rest", 0), ("keys", 0), ("hop", 0), ("hop", 1)]
    + [("pass", j) for j in range(J)]
    + [("even rest", 0), ("hop", 2), ("hop", 3)]
    + [("hop_pair", j) for j in range(J)]
    + [("weights", i) for i in range(NK, NW)]
)


def kernel(
    base, local, moment, exps, acts, gain,
    base_out, moment_out, keys_out,
    bbuf, qbuf, ebuf, mbuf, xbuf, gbuf, wbuf, vbuf, sbuf, dbuf, pbuf, zbuf, nbuf, acc, kbuf,
    load_b, load_q, load_e, load_m, load_x, store_n, store_m,
    g_send, g_recv, w_send, w_recv, f_send, f_recv, v_send, v_recv, s_send, s_recv, d_send, d_recv,
    z_send, z_recv, a_send, a_recv, n_send, n_recv, h_send, h_recv, k_send, k_recv,
):
    r, s, t = lax.axis_index("replica"), lax.axis_index("section"), lax.axis_index("tensor")
    x, zl = r // 2, r % 2
    before, after = (r, (s + 7) % 8, t), (r, (s + 1) % 8, t)
    sibling = (r, s, 1 - t)
    rz = x * 2 + 1 - zl
    pair = (rz, s, t)
    up, down = ((x + 1) % 4) * 2 + zl, ((x + 3) % 4) * 2 + zl
    along = [(up, s, t), (down, s, t)]

    def rows(j):
        return pl.ds(j * JR, JR)

    def remote(src, dst, send, recv, to):
        return pltpu.make_async_remote_copy(
            src_ref=src, dst_ref=dst, send_sem=send, recv_sem=recv, device_id=to, device_id_type=MESH
        )

    def weights_copy(i):
        b, k = i // NK, i % NK
        cols = pl.ds(pl.multiple_of(b * LANES, LANES), LANES)
        deep = pl.ds(pl.multiple_of(k * KR, KR), KR)
        return remote(local.at[deep, cols], wbuf.at[b, t, deep], w_send.at[i], w_recv.at[i], before)

    def share_copy(i, core):
        b, k = i // NK, i % NK
        deep = pl.ds(pl.multiple_of(k * KR, KR), KR)
        ref = wbuf.at[b, core, deep]
        return remote(ref, ref, f_send.at[i], f_recv.at[i], sibling)

    gain_copy = remote(gain, gbuf, g_send, g_recv, before)

    def shard(d):
        return (x + d) % 4 * 2

    def via_copy(j, h):
        return remote(
            qbuf.at[shard(2) + h, rows(j)], vbuf.at[h, rows(j)], v_send.at[h, j], v_recv.at[h, j], along[h]
        )

    def sum_copy(j, h):
        return remote(vbuf.at[h, rows(j)], sbuf.at[h, rows(j)], s_send.at[h, j], s_recv.at[h, j], along[h])

    def term_copy(j, h):
        return remote(
            qbuf.at[shard(3 if h == 0 else 1) + h, rows(j)], dbuf.at[h, rows(j)],
            d_send.at[h, j], d_recv.at[h, j], along[1 - h],
        )

    def half_copy(j):
        return remote(pbuf.at[1 - zl, rows(j)], zbuf.at[rows(j)], z_send.at[j], z_recv.at[j], pair)

    def pair_copy(j):
        return remote(nbuf.at[rows(j)], base_out.at[r, rows(j)], a_send.at[j], a_recv.at[j], pair)

    def own_copy(j, w):
        return remote(
            nbuf.at[rows(j)], base_out.at[r, rows(j)], n_send.at[zl, w, j], n_recv.at[zl, w, j], along[w]
        )

    def pass_copy(j, w):
        ref = base_out.at[rz, rows(j)]
        return remote(ref, ref, n_send.at[1 - zl, w, j], n_recv.at[1 - zl, w, j], along[w])

    def came_copy(j, h, w):
        ref = base_out.at[(x + 3 + 2 * w) % 4 * 2 + h, rows(j)]
        return remote(ref, ref, n_send.at[h, w, j], n_recv.at[h, w, j], along[0])

    def hop_copy(j, h):
        ref = base_out.at[(x + 3 + 2 * h) % 4 * 2 + h, rows(j)]
        to = ((x + 1 + 2 * h) % 4 * 2 + zl, s, t)
        return remote(ref, ref, h_send.at[h, j], h_recv.at[h, j], to)

    def key_copy(b, c):
        return remote(
            kbuf.at[b, c], keys_out.at[:, pl.ds(c * KV + b * LANES, LANES)],
            k_send.at[b, c], k_recv.at[b, c], after,
        )

    def store_copy(j):
        return pltpu.make_async_copy(nbuf.at[rows(j)], base_out.at[r, rows(j)], store_n.at[j])

    store_moment = pltpu.make_async_copy(mbuf, moment_out, store_m)

    def load_base(j):
        return pltpu.make_async_copy(base.at[:, rows(j)], bbuf.at[:, rows(j)], load_b.at[j])

    local3 = local.reshape(REPLICAS, ROWS, KV)

    def load_local(j):
        return pltpu.make_async_copy(local3.at[:, rows(j)], qbuf.at[:, rows(j)], load_q.at[j])

    load_exps = pltpu.make_async_copy(exps, ebuf, load_e)
    load_moment = pltpu.make_async_copy(moment, mbuf, load_m)

    def load_acts(i):
        part = pl.ds(i * XR, XR)
        return pltpu.make_async_copy(acts.at[part], xbuf.at[part], load_x.at[i])

    load_exps.start()
    for j in range(J):
        load_base(j).start()
        load_local(j).start()

    barrier = pltpu.get_barrier_semaphore()
    for peer in (before, after, sibling, pair, *along):
        pl.semaphore_signal(barrier, inc=1, device_id=peer, device_id_type=MESH)
    pl.semaphore_wait(barrier, 6)

    gain_copy.start()

    @pl.loop(0, EARLY)
    def _(i):
        weights_copy(i).start()

    load_exps.wait()
    for j in range(J):
        load_base(j).wait()
        load_local(j).wait()

        @pl.loop(0, REPLICAS)
        def _(q):
            e = ebuf[q, pl.ds(j * (JR // 32), JR // 32), :]
            scale = jnp.where(e < 0, 0.5, jnp.where(e > 0, 2.0, 1.0)).astype(jnp.float32)
            inverse = jnp.where(e < 0, 2.0, jnp.where(e > 0, 0.5, 1.0)).astype(jnp.float32)
            delta = bbuf[q, rows(j), :].astype(jnp.float32) - qbuf[q, rows(j), :].astype(jnp.float32)
            y = delta.reshape(JR // 32, 32, KV) * inverse[:, None, :]
            a = jnp.minimum(jnp.abs(y), 6.0)
            spacing = jnp.where(a < 2.0, 0.5, jnp.where(a < 4.0, 1.0, 2.0))
            per = jnp.where(a < 2.0, 2.0, jnp.where(a < 4.0, 1.0, 0.5))
            level = jnp.floor(a * per + 0.5) * spacing * scale[:, None, :]
            level = jnp.where(y < 0.0, -level, level)
            qbuf[q, rows(j), :] = level.reshape(JR, KV).astype(jnp.bfloat16)

        for h in range(2):
            via_copy(j, h).start()
        for h in range(2):
            term_copy(j, h).start()
        if j == 1:
            for i in range(XP):
                load_acts(i).start()
            load_moment.start()

    def normalize(part_at):
        load_acts(part_at).wait()
        if part_at == 0:
            gain_copy.wait_recv()

        @pl.loop(0, XR // NR)
        def _(i):
            part = pl.ds(pl.multiple_of(part_at * XR + i * NR, NR), NR)
            total = jnp.zeros((NR, LANES), jnp.float32)
            for k in range(NK):
                v = xbuf[part, k * KR : (k + 1) * KR].astype(jnp.float32)
                v = v * v
                for lane in range(0, KR, LANES):
                    total = total + v[:, lane : lane + LANES]
            meansq = jnp.sum(total, axis=-1, keepdims=True) * (1.0 / D)
            factor = lax.rsqrt(meansq + NORM_EPSILON)
            for k in range(NK):
                cols = slice(k * KR, (k + 1) * KR)
                v = xbuf[part, cols].astype(jnp.float32)
                xbuf[part, cols] = (v * factor * gbuf[:, cols]).astype(jnp.bfloat16)

    def relay(j):
        for h in range(2):
            via_copy(j, h).wait_recv()
            mine = qbuf[shard(1 if h == 0 else 3) + h, rows(j), :].astype(jnp.float32)
            vbuf[h, rows(j), :] = (vbuf[h, rows(j), :].astype(jnp.float32) + mine).astype(jnp.bfloat16)
            sum_copy(j, h).start()

    def sum_terms(j):
        for h in range(2):
            term_copy(j, h).wait_recv()
            sum_copy(j, h).wait_recv()
            total = qbuf[x * 2 + h, rows(j), :].astype(jnp.float32)
            total = total + sbuf[h, rows(j), :].astype(jnp.float32) + dbuf[h, rows(j), :].astype(jnp.float32)
            pbuf[h, rows(j), :] = total.astype(jnp.bfloat16)
        half_copy(j).start()

    def update(j):
        if j == 0:
            load_moment.wait()
        half_copy(j).wait_recv()
        total = pbuf[zl, rows(j), :].astype(jnp.float32) + zbuf[rows(j), :].astype(jnp.float32)
        pseudo = total * (1.0 / REPLICAS)
        new = MOMENTUM_DECAY * mbuf[rows(j), :] + pseudo
        mbuf[rows(j), :] = new
        old = bbuf[r, rows(j), :].astype(jnp.float32)
        nbuf[rows(j), :] = (old - OUTER_RATE * (pseudo + MOMENTUM_DECAY * new)).astype(jnp.bfloat16)
        pair_copy(j).start()
        for w in range(2):
            own_copy(j, w).start()
        store_copy(j).start()
        if j == J - 1:
            store_moment.start()

    def pass_on(j):
        pair_copy(j).wait_recv()
        for w in range(2):
            pass_copy(j, w).start()

    def hop(j, h):
        came_copy(j, h, h).wait_recv()
        hop_copy(j, h).start()

    def weights(i):
        weights_copy(i).wait_recv()
        share_copy(i, t).start()

    def multiply(i):
        share_copy(i, 1 - t).wait_recv()
        b, k = i // NK, i % NK
        deep = pl.ds(pl.multiple_of(k * KR, KR), KR)

        @pl.loop(0, TOK // MR)
        def _(m):
            part = pl.ds(pl.multiple_of(m * MR, MR), MR)
            w = jnp.concatenate([wbuf[b, 0, deep, :], wbuf[b, 1, deep, :]], axis=1)
            product = jnp.dot(xbuf[part, deep], w, preferred_element_type=jnp.float32)
            kept = jnp.where(k == 0, 0.0, acc[part, :])
            acc[part, :] = kept + product

    def arrive(first, last):
        if first % NK == 0:
            weights(first)
            first += 1

        @pl.loop(first, last)
        def _(i):
            weights(i)
            multiply(i - 1)

    def keys(b):
        for c in range(2):
            kbuf[b, c] = (acc[:, c * LANES : (c + 1) * LANES] * D ** (-0.5)).astype(jnp.bfloat16)
            key_copy(b, c).start()

    run = []

    def flush():
        if run:
            arrive(run[0], run[-1] + 1)
            run.clear()

    for name, i in ORDER:
        if name == "weights":
            run.append(i)
            if i % NK == NK - 1:
                flush()
            continue
        flush()
        if name in ("odd rest", "even rest"):

            @pl.when(s % 2 == (1 if name == "odd rest" else 0))
            def _():
                @pl.loop(EARLY, NW)
                def _(k):
                    weights_copy(k).start()

        elif name == "keys":
            multiply(NK - 1)
            keys(0)
        elif name == "hop":
            hop(i, zl)
        elif name == "hop_pair":
            hop(i, 1 - zl)
        else:
            {"normalize": normalize, "relay": relay, "sum": sum_terms, "update": update, "pass": pass_on}[name](i)
    flush()
    multiply(NW - 1)
    keys(1)

    gain_copy.wait_send()

    @pl.loop(0, NW)
    def _(i):
        weights_copy(i).wait_send()
        share_copy(i, t).wait_send()

    @pl.loop(0, J)
    def _(j):
        half_copy(j).wait_send()
        pair_copy(j).wait_send()
        store_copy(j).wait()
        for h in range(2):
            via_copy(j, h).wait_send()
            sum_copy(j, h).wait_send()
            term_copy(j, h).wait_send()
            own_copy(j, h).wait_send()
            pass_copy(j, h).wait_send()
            came_copy(j, h, 1 - h).wait_recv()
            hop_copy(j, h).wait()

    store_moment.wait()
    for b in range(2):
        for c in range(2):
            key_copy(b, c).wait()


def hand_on(base, moment, keys, base_out, moment_out, keys_out, base_held, moment_held, keys_held, came, left):
    parts = [(base.at[i], base_held.at[i], base_out.at[i]) for i in range(REPLICAS)]
    for i in range(2):
        part = pl.ds(i * (ROWS // 2), ROWS // 2)
        parts.append((moment.at[part], moment_held.at[part], moment_out.at[part]))
    parts.append((keys, keys_held, keys_out))
    reads = [pltpu.make_async_copy(src, held, came.at[i]) for i, (src, held, _) in enumerate(parts)]
    writes = [pltpu.make_async_copy(held, dst, left.at[i]) for i, (_, held, dst) in enumerate(parts)]
    for read in reads:
        read.start()
    for read, write in zip(reads, writes):
        read.wait()
        write.start()
    for write in writes:
        write.wait()


def shards(base_weights, local_weights, outer_momentum, scale_exponents, section_inputs, norm_gain):
    bf16, f32 = jnp.bfloat16, jnp.float32
    hbm = pl.BlockSpec(memory_space=pl.ANY)
    dma = pltpu.SemaphoreType.DMA
    new_base, new_moment, keys = pl.pallas_call(
        kernel,
        out_shape=(
            jax.ShapeDtypeStruct((REPLICAS, ROWS, KV), bf16),
            jax.ShapeDtypeStruct((ROWS, KV), f32),
            jax.ShapeDtypeStruct((TOK, 2 * KV), bf16),
        ),
        in_specs=[hbm] * 6,
        out_specs=(hbm, hbm, hbm),
        scratch_shapes=[
            pltpu.VMEM((REPLICAS, ROWS, KV), bf16),
            pltpu.VMEM((REPLICAS, ROWS, KV), bf16),
            pltpu.VMEM((REPLICAS, ROWS // 32, KV), jnp.int32),
            pltpu.VMEM((ROWS, KV), f32),
            pltpu.VMEM((TOK, D), bf16),
            pltpu.VMEM((1, D), f32),
            pltpu.VMEM((2, 2, D, LANES), bf16),
            pltpu.VMEM((2, ROWS, KV), bf16),
            pltpu.VMEM((2, ROWS, KV), bf16),
            pltpu.VMEM((2, ROWS, KV), bf16),
            pltpu.VMEM((2, ROWS, KV), bf16),
            pltpu.VMEM((ROWS, KV), bf16),
            pltpu.VMEM((ROWS, KV), bf16),
            pltpu.VMEM((TOK, KV), f32),
            pltpu.VMEM((2, 2, TOK, LANES), bf16),
            dma((J,)), dma((J,)), dma, dma, dma((XP,)), dma((J,)), dma,
            dma, dma, dma((NW,)), dma((NW,)), dma((NW,)), dma((NW,)),
            dma((2, J)), dma((2, J)), dma((2, J)), dma((2, J)), dma((2, J)), dma((2, J)),
            dma((J,)), dma((J,)), dma((J,)), dma((J,)), dma((2, 2, J)), dma((2, 2, J)), dma((2, J)), dma((2, J)),
            dma((2, 2)), dma((2, 2)),
        ],
        compiler_params=pltpu.CompilerParams(
            collective_id=0, has_side_effects=True, vmem_limit_bytes=56 << 20
        ),
        cost_estimate=pl.CostEstimate(
            flops=2 * TOK * D * 2 * KV, bytes_accessed=40 << 20, transcendentals=0
        ),
    )(
        base_weights.reshape(REPLICAS, ROWS, KV),
        local_weights.reshape(D, KV),
        outer_momentum.reshape(ROWS, KV),
        scale_exponents.reshape(REPLICAS, ROWS // 32, KV),
        section_inputs.reshape(TOK, D),
        norm_gain,
    )
    outs = (new_base, new_moment, keys)
    new_base, new_moment, keys = pl.pallas_call(
        hand_on,
        out_shape=tuple(jax.ShapeDtypeStruct(out.shape, out.dtype) for out in outs),
        in_specs=[hbm] * 3,
        out_specs=(hbm,) * 3,
        scratch_shapes=[pltpu.VMEM(out.shape, out.dtype) for out in outs] + [dma((REPLICAS + 3,))] * 2,
        compiler_params=pltpu.CompilerParams(vmem_limit_bytes=60 << 20),
        cost_estimate=pl.CostEstimate(flops=0, bytes_accessed=12 << 20, transcendentals=0),
    )(*outs)
    return (
        new_base.reshape(1, D, KV),
        new_moment.reshape(1, ROWS, KV),
        keys.reshape(1, 1, TOK, 2 * KV),
    )


def solution(mesh):
    placed = (
        P("section", None, "tensor"),
        P("replica", "section", None, "tensor"),
        P("section", "replica", "tensor"),
        P("section", None, "tensor"),
        P("replica", "section", "tensor", None),
        P("section", None),
    )
    return jax.shard_map(
        shards,
        mesh=mesh,
        in_specs=placed,
        out_specs=(
            P("section", None, "tensor"),
            P("section", "replica", "tensor"),
            P("replica", "section", "tensor", None),
        ),
        check_vma=False,
    )
```

```python
import jax
import jax.numpy as jnp
from jax import lax
from jax.experimental import pallas as pl
from jax.experimental.pallas import tpu as pltpu
from jax.sharding import PartitionSpec as P

MESH = pl.DeviceIdType.MESH
D = 8192
TOK = 640
KV = 256
LANES = 128
REPLICAS = 8
ROWS = D // REPLICAS
J = 4
JR = ROWS // J
NK = 8
KR = D // NK
NW = 2 * NK
XP = 4
XR = TOK // XP
NR = 32
MR = TOK // 2

OUTER_RATE = 0.7
MOMENTUM_DECAY = 0.9
NORM_EPSILON = 1e-05


EARLY = 8
ORDER = (
    [("relay", 0), ("normalize", 0), ("normalize", 1), ("sum", 0), ("normalize", 2), ("normalize", 3)]
    + [("relay", 1), ("sum", 1), ("weights", 0), ("weights", 1)]
    + [("relay", 2), ("sum", 2), ("weights", 2), ("weights", 3), ("relay", 3), ("sum", 3)]
    + [("weights", i) for i in range(4, NK)]
    + [("update", j) for j in range(J)]
    + [("odd rest", 0), ("keys", 0), ("hop", 0), ("hop", 1)]
    + [("pass", j) for j in range(J)]
    + [("even rest", 0), ("hop", 2), ("hop", 3)]
    + [("hop_pair", j) for j in range(J)]
    + [("weights", i) for i in range(NK, NW)]
)


def kernel(
    base, local, moment, exps, acts, gain,
    base_out, moment_out, keys_out,
    bbuf, qbuf, ebuf, mbuf, xbuf, gbuf, wbuf, vbuf, sbuf, dbuf, pbuf, zbuf, nbuf, acc, kbuf,
    load_b, load_q, load_e, load_m, load_x, store_n, store_m,
    g_send, g_recv, w_send, w_recv, f_send, f_recv, v_send, v_recv, s_send, s_recv, d_send, d_recv,
    z_send, z_recv, a_send, a_recv, n_send, n_recv, h_send, h_recv, k_send, k_recv,
):
    r, s, t = lax.axis_index("replica"), lax.axis_index("section"), lax.axis_index("tensor")
    x, zl = r // 2, r % 2
    before, after = (r, (s + 7) % 8, t), (r, (s + 1) % 8, t)
    sibling = (r, s, 1 - t)
    rz = x * 2 + 1 - zl
    pair = (rz, s, t)
    up, down = ((x + 1) % 4) * 2 + zl, ((x + 3) % 4) * 2 + zl
    along = [(up, s, t), (down, s, t)]

    def rows(j):
        return pl.ds(j * JR, JR)

    def remote(src, dst, send, recv, to):
        return pltpu.make_async_remote_copy(
            src_ref=src, dst_ref=dst, send_sem=send, recv_sem=recv, device_id=to, device_id_type=MESH
        )

    def weights_copy(i):
        b, k = i // NK, i % NK
        cols = pl.ds(pl.multiple_of(b * LANES, LANES), LANES)
        deep = pl.ds(pl.multiple_of(k * KR, KR), KR)
        return remote(local.at[deep, cols], wbuf.at[b, t, deep], w_send.at[i], w_recv.at[i], before)

    def share_copy(i, core):
        b, k = i // NK, i % NK
        deep = pl.ds(pl.multiple_of(k * KR, KR), KR)
        ref = wbuf.at[b, core, deep]
        return remote(ref, ref, f_send.at[i], f_recv.at[i], sibling)

    gain_copy = remote(gain, gbuf, g_send, g_recv, before)

    def shard(d):
        return (x + d) % 4 * 2

    def via_copy(j, h):
        return remote(
            qbuf.at[shard(2) + h, rows(j)], vbuf.at[h, rows(j)], v_send.at[h, j], v_recv.at[h, j], along[h]
        )

    def sum_copy(j, h):
        return remote(vbuf.at[h, rows(j)], sbuf.at[h, rows(j)], s_send.at[h, j], s_recv.at[h, j], along[h])

    def term_copy(j, h):
        return remote(
            qbuf.at[shard(3 if h == 0 else 1) + h, rows(j)], dbuf.at[h, rows(j)],
            d_send.at[h, j], d_recv.at[h, j], along[1 - h],
        )

    def half_copy(j):
        return remote(pbuf.at[1 - zl, rows(j)], zbuf.at[rows(j)], z_send.at[j], z_recv.at[j], pair)

    def pair_copy(j):
        return remote(nbuf.at[rows(j)], base_out.at[r, rows(j)], a_send.at[j], a_recv.at[j], pair)

    def own_copy(j, w):
        return remote(
            nbuf.at[rows(j)], base_out.at[r, rows(j)], n_send.at[zl, w, j], n_recv.at[zl, w, j], along[w]
        )

    def pass_copy(j, w):
        ref = base_out.at[rz, rows(j)]
        return remote(ref, ref, n_send.at[1 - zl, w, j], n_recv.at[1 - zl, w, j], along[w])

    def came_copy(j, h, w):
        ref = base_out.at[(x + 3 + 2 * w) % 4 * 2 + h, rows(j)]
        return remote(ref, ref, n_send.at[h, w, j], n_recv.at[h, w, j], along[0])

    def hop_copy(j, h):
        ref = base_out.at[(x + 3 + 2 * h) % 4 * 2 + h, rows(j)]
        to = ((x + 1 + 2 * h) % 4 * 2 + zl, s, t)
        return remote(ref, ref, h_send.at[h, j], h_recv.at[h, j], to)

    def key_copy(b, c):
        return remote(
            kbuf.at[b, c], keys_out.at[:, pl.ds(c * KV + b * LANES, LANES)],
            k_send.at[b, c], k_recv.at[b, c], after,
        )

    def store_copy(j):
        return pltpu.make_async_copy(nbuf.at[rows(j)], base_out.at[r, rows(j)], store_n.at[j])

    store_moment = pltpu.make_async_copy(mbuf, moment_out, store_m)

    def load_base(j):
        return pltpu.make_async_copy(base.at[:, rows(j)], bbuf.at[:, rows(j)], load_b.at[j])

    local3 = local.reshape(REPLICAS, ROWS, KV)

    def load_local(j):
        return pltpu.make_async_copy(local3.at[:, rows(j)], qbuf.at[:, rows(j)], load_q.at[j])

    load_exps = pltpu.make_async_copy(exps, ebuf, load_e)
    load_moment = pltpu.make_async_copy(moment, mbuf, load_m)

    def load_acts(i):
        part = pl.ds(i * XR, XR)
        return pltpu.make_async_copy(acts.at[part], xbuf.at[part], load_x.at[i])

    barrier = pltpu.get_barrier_semaphore()
    for peer in (before, after, sibling, pair, *along):
        pl.semaphore_signal(barrier, inc=1, device_id=peer, device_id_type=MESH)

    load_exps.start()
    for j in range(J):
        load_base(j).start()
        load_local(j).start()

    pl.semaphore_wait(barrier, 6)

    gain_copy.start()

    @pl.loop(0, EARLY)
    def _(i):
        weights_copy(i).start()

    load_exps.wait()
    for j in range(J):
        load_base(j).wait()
        load_local(j).wait()

        @pl.loop(0, REPLICAS)
        def _(q):
            e = ebuf[q, pl.ds(j * (JR // 32), JR // 32), :]
            scale = jnp.where(e < 0, 0.5, jnp.where(e > 0, 2.0, 1.0)).astype(jnp.float32)
            inverse = jnp.where(e < 0, 2.0, jnp.where(e > 0, 0.5, 1.0)).astype(jnp.float32)
            delta = bbuf[q, rows(j), :].astype(jnp.float32) - qbuf[q, rows(j), :].astype(jnp.float32)
            y = delta.reshape(JR // 32, 32, KV) * inverse[:, None, :]
            a = jnp.minimum(jnp.abs(y), 6.0)
            spacing = jnp.where(a < 2.0, 0.5, jnp.where(a < 4.0, 1.0, 2.0))
            per = jnp.where(a < 2.0, 2.0, jnp.where(a < 4.0, 1.0, 0.5))
            level = jnp.floor(a * per + 0.5) * spacing * scale[:, None, :]
            level = jnp.where(y < 0.0, -level, level)
            qbuf[q, rows(j), :] = level.reshape(JR, KV).astype(jnp.bfloat16)

        for h in range(2):
            via_copy(j, h).start()
        for h in range(2):
            term_copy(j, h).start()
        if j == 1:
            for i in range(XP):
                load_acts(i).start()
            load_moment.start()

    def normalize(part_at):
        load_acts(part_at).wait()
        if part_at == 0:
            gain_copy.wait_recv()

        @pl.loop(0, XR // NR)
        def _(i):
            part = pl.ds(pl.multiple_of(part_at * XR + i * NR, NR), NR)
            total = jnp.zeros((NR, LANES), jnp.float32)
            for k in range(NK):
                v = xbuf[part, k * KR : (k + 1) * KR].astype(jnp.float32)
                v = v * v
                for lane in range(0, KR, LANES):
                    total = total + v[:, lane : lane + LANES]
            meansq = jnp.sum(total, axis=-1, keepdims=True) * (1.0 / D)
            factor = lax.rsqrt(meansq + NORM_EPSILON)
            for k in range(NK):
                cols = slice(k * KR, (k + 1) * KR)
                v = xbuf[part, cols].astype(jnp.float32)
                xbuf[part, cols] = (v * factor * gbuf[:, cols]).astype(jnp.bfloat16)

    def relay(j):
        for h in range(2):
            via_copy(j, h).wait_recv()
            mine = qbuf[shard(1 if h == 0 else 3) + h, rows(j), :].astype(jnp.float32)
            vbuf[h, rows(j), :] = (vbuf[h, rows(j), :].astype(jnp.float32) + mine).astype(jnp.bfloat16)
            sum_copy(j, h).start()

    def sum_terms(j):
        for h in range(2):
            term_copy(j, h).wait_recv()
            sum_copy(j, h).wait_recv()
            total = qbuf[x * 2 + h, rows(j), :].astype(jnp.float32)
            total = total + sbuf[h, rows(j), :].astype(jnp.float32) + dbuf[h, rows(j), :].astype(jnp.float32)
            pbuf[h, rows(j), :] = total.astype(jnp.bfloat16)
        half_copy(j).start()

    def update(j):
        if j == 0:
            load_moment.wait()
        half_copy(j).wait_recv()
        total = pbuf[zl, rows(j), :].astype(jnp.float32) + zbuf[rows(j), :].astype(jnp.float32)
        pseudo = total * (1.0 / REPLICAS)
        new = MOMENTUM_DECAY * mbuf[rows(j), :] + pseudo
        mbuf[rows(j), :] = new
        old = bbuf[r, rows(j), :].astype(jnp.float32)
        nbuf[rows(j), :] = (old - OUTER_RATE * (pseudo + MOMENTUM_DECAY * new)).astype(jnp.bfloat16)
        pair_copy(j).start()
        for w in range(2):
            own_copy(j, w).start()
        store_copy(j).start()
        if j == J - 1:
            store_moment.start()

    def pass_on(j):
        pair_copy(j).wait_recv()
        for w in range(2):
            pass_copy(j, w).start()

    def hop(j, h):
        came_copy(j, h, h).wait_recv()
        hop_copy(j, h).start()

    def weights(i):
        weights_copy(i).wait_recv()
        share_copy(i, t).start()

    def multiply(i):
        share_copy(i, 1 - t).wait_recv()
        b, k = i // NK, i % NK
        deep = pl.ds(pl.multiple_of(k * KR, KR), KR)

        @pl.loop(0, TOK // MR)
        def _(m):
            part = pl.ds(pl.multiple_of(m * MR, MR), MR)
            w = jnp.concatenate([wbuf[b, 0, deep, :], wbuf[b, 1, deep, :]], axis=1)
            product = jnp.dot(xbuf[part, deep], w, preferred_element_type=jnp.float32)
            kept = jnp.where(k == 0, 0.0, acc[part, :])
            acc[part, :] = kept + product

    def arrive(first, last):
        if first % NK == 0:
            weights(first)
            first += 1

        @pl.loop(first, last)
        def _(i):
            weights(i)
            multiply(i - 1)

    def keys(b):
        for c in range(2):
            kbuf[b, c] = (acc[:, c * LANES : (c + 1) * LANES] * D ** (-0.5)).astype(jnp.bfloat16)
            key_copy(b, c).start()

    run = []

    def flush():
        if run:
            arrive(run[0], run[-1] + 1)
            run.clear()

    for name, i in ORDER:
        if name == "weights":
            run.append(i)
            if i % NK == NK - 1:
                flush()
            continue
        flush()
        if name in ("odd rest", "even rest"):

            @pl.when(s % 2 == (1 if name == "odd rest" else 0))
            def _():
                @pl.loop(EARLY, NW)
                def _(k):
                    weights_copy(k).start()

        elif name == "keys":
            multiply(NK - 1)
            keys(0)
        elif name == "hop":
            hop(i, zl)
        elif name == "hop_pair":
            hop(i, 1 - zl)
        else:
            {"normalize": normalize, "relay": relay, "sum": sum_terms, "update": update, "pass": pass_on}[name](i)
    flush()
    multiply(NW - 1)
    keys(1)

    gain_copy.wait_send()

    @pl.loop(0, NW)
    def _(i):
        weights_copy(i).wait_send()
        share_copy(i, t).wait_send()

    @pl.loop(0, J)
    def _(j):
        half_copy(j).wait_send()
        pair_copy(j).wait_send()
        store_copy(j).wait()
        for h in range(2):
            via_copy(j, h).wait_send()
            sum_copy(j, h).wait_send()
            term_copy(j, h).wait_send()
            own_copy(j, h).wait_send()
            pass_copy(j, h).wait_send()
            came_copy(j, h, 1 - h).wait_recv()
            hop_copy(j, h).wait()

    store_moment.wait()
    for b in range(2):
        for c in range(2):
            key_copy(b, c).wait()


def hand_on(base, moment, keys, base_out, moment_out, keys_out, base_held, moment_held, keys_held, came, left):
    parts = [(base.at[i], base_held.at[i], base_out.at[i]) for i in range(REPLICAS)]
    for i in range(2):
        part = pl.ds(i * (ROWS // 2), ROWS // 2)
        parts.append((moment.at[part], moment_held.at[part], moment_out.at[part]))
    parts.append((keys, keys_held, keys_out))
    reads = [pltpu.make_async_copy(src, held, came.at[i]) for i, (src, held, _) in enumerate(parts)]
    writes = [pltpu.make_async_copy(held, dst, left.at[i]) for i, (_, held, dst) in enumerate(parts)]
    for read in reads:
        read.start()
    for read, write in zip(reads, writes):
        read.wait()
        write.start()
    for write in writes:
        write.wait()


def shards(base_weights, local_weights, outer_momentum, scale_exponents, section_inputs, norm_gain):
    bf16, f32 = jnp.bfloat16, jnp.float32
    hbm = pl.BlockSpec(memory_space=pl.ANY)
    dma = pltpu.SemaphoreType.DMA
    new_base, new_moment, keys = pl.pallas_call(
        kernel,
        out_shape=(
            jax.ShapeDtypeStruct((REPLICAS, ROWS, KV), bf16),
            jax.ShapeDtypeStruct((ROWS, KV), f32),
            jax.ShapeDtypeStruct((TOK, 2 * KV), bf16),
        ),
        in_specs=[hbm] * 6,
        out_specs=(hbm, hbm, hbm),
        scratch_shapes=[
            pltpu.VMEM((REPLICAS, ROWS, KV), bf16),
            pltpu.VMEM((REPLICAS, ROWS, KV), bf16),
            pltpu.VMEM((REPLICAS, ROWS // 32, KV), jnp.int32),
            pltpu.VMEM((ROWS, KV), f32),
            pltpu.VMEM((TOK, D), bf16),
            pltpu.VMEM((1, D), f32),
            pltpu.VMEM((2, 2, D, LANES), bf16),
            pltpu.VMEM((2, ROWS, KV), bf16),
            pltpu.VMEM((2, ROWS, KV), bf16),
            pltpu.VMEM((2, ROWS, KV), bf16),
            pltpu.VMEM((2, ROWS, KV), bf16),
            pltpu.VMEM((ROWS, KV), bf16),
            pltpu.VMEM((ROWS, KV), bf16),
            pltpu.VMEM((TOK, KV), f32),
            pltpu.VMEM((2, 2, TOK, LANES), bf16),
            dma((J,)), dma((J,)), dma, dma, dma((XP,)), dma((J,)), dma,
            dma, dma, dma((NW,)), dma((NW,)), dma((NW,)), dma((NW,)),
            dma((2, J)), dma((2, J)), dma((2, J)), dma((2, J)), dma((2, J)), dma((2, J)),
            dma((J,)), dma((J,)), dma((J,)), dma((J,)), dma((2, 2, J)), dma((2, 2, J)), dma((2, J)), dma((2, J)),
            dma((2, 2)), dma((2, 2)),
        ],
        compiler_params=pltpu.CompilerParams(
            collective_id=0, has_side_effects=True, vmem_limit_bytes=56 << 20
        ),
        cost_estimate=pl.CostEstimate(
            flops=2 * TOK * D * 2 * KV, bytes_accessed=40 << 20, transcendentals=0
        ),
    )(
        base_weights.reshape(REPLICAS, ROWS, KV),
        local_weights.reshape(D, KV),
        outer_momentum.reshape(ROWS, KV),
        scale_exponents.reshape(REPLICAS, ROWS // 32, KV),
        section_inputs.reshape(TOK, D),
        norm_gain,
    )
    outs = (new_base, new_moment, keys)
    new_base, new_moment, keys = pl.pallas_call(
        hand_on,
        out_shape=tuple(jax.ShapeDtypeStruct(out.shape, out.dtype) for out in outs),
        in_specs=[hbm] * 3,
        out_specs=(hbm,) * 3,
        scratch_shapes=[pltpu.VMEM(out.shape, out.dtype) for out in outs] + [dma((REPLICAS + 3,))] * 2,
        compiler_params=pltpu.CompilerParams(vmem_limit_bytes=60 << 20),
        cost_estimate=pl.CostEstimate(flops=0, bytes_accessed=12 << 20, transcendentals=0),
    )(*outs)
    return (
        new_base.reshape(1, D, KV),
        new_moment.reshape(1, ROWS, KV),
        keys.reshape(1, 1, TOK, 2 * KV),
    )


def solution(mesh):
    placed = (
        P("section", None, "tensor"),
        P("replica", "section", None, "tensor"),
        P("section", "replica", "tensor"),
        P("section", None, "tensor"),
        P("replica", "section", "tensor", None),
        P("section", None),
    )
    return jax.shard_map(
        shards,
        mesh=mesh,
        in_specs=placed,
        out_specs=(
            P("section", None, "tensor"),
            P("section", "replica", "tensor"),
            P("replica", "section", "tensor", None),
        ),
        check_vma=False,
    )
```
